32 devices in a mesh: groups: 2 (over y), img: 4 (over z), samp: 2 (over x), sub: 2 (over core).
Axes of the slice: x: 2, y: 2, z: 4, core: 2. Of those that a mesh axis runs over, the one named last changes fastest.
Arguments:
- images: bfloat16 [2, 4096, 16384], P(None, ('groups', 'img'), ('samp', 'sub')), parts along dimension 1, may hold values from -6 to 6
- references: bfloat16 [2, 32, 16384], P(None, 'img', ('samp', 'sub')), may hold values from -0.03125 to 0.03125
- noise_weight: float32 [16384], P(('samp', 'sub')), may hold values from 0.3 to 3
- normalizer: float32 [4096], P(('groups', 'img')), parts along dimension 0, may hold values from -1 to 1
- owner_order: int32 [32], replicated, may hold values from 0 to 31, each once
Outputs:
- weighted_sums: bfloat16 [32, 4, 16384], P('img', 'groups', ('samp', 'sub')), parts along dimension 1
The draws below stay inside these ranges and needn't reach their ends.
There are 2 independent parts, one for each index of `groups`. The reference program is written for one: setup_inputs(seed, part) draws one part's arguments, and reference() takes and returns one part's arrays. A program takes and returns all parts, laid end to end along the dimension named above; an argument that names none is the same for every part. Nothing has to cross between parts.
Inputs may be any that keep to these rules, and one draw needn't show every extreme that they name: `owner_order`: each orientation appears exactly once.
All inputs are finite; a program needn't handle non-finite values.
Results may differ from the reference program's by a relative error of at most 0.012.
The reference program's roundings to bfloat16 on the way (of `weighted_refs` and `posterior`) count: a program that leaves them out, or rounds other values in their place, can miss the bound.
Values may be sent and summed in bfloat16 or wider, within the bound.
A program may use at most 64 MiB of HBM per device.

```python
import math
import jax
import jax.numpy as jnp
from jax import lax

S = 16384
IMAGES = 2048
ORIENT = 32


def levels(rng, dims, cuts, smallest, top_value):
    def one(axis_at, shards_of):
        steps = jax.random.uniform(jax.random.fold_in(jax.random.fold_in(rng, 6), axis_at), (shards_of,), jnp.float32, smallest / len(cuts), top_value / len(cuts))
        return jnp.repeat(jnp.exp(steps), dims[axis_at] // shards_of).reshape((-1,) + (1,) * (len(dims) - axis_at - 1))

    level = one(*cuts[0])
    for cut in cuts[1:]:
        level = level * one(*cut)
    return level


def noise(own_key, shape, scale, limit, shards=(), dtype=jnp.bfloat16):
    drawn = scale * jax.random.normal(own_key, shape, jnp.float32)
    if shards:
        drawn = drawn * levels(own_key, shape, shards, -0.22, 0.18)
    return jnp.clip(drawn, -limit, limit).astype(dtype)


def setup_inputs(seed: int = 0, part: int = 0) -> dict:
    key_list = jax.random.split(jax.random.key(seed), 6)
    own_keys = jax.random.split(jax.random.fold_in(key_list[5], part), 6)
    return {
        "images": noise(own_keys[0], (2, IMAGES, S), 1.0, 6.0, ((1, 4), (2, 4))),
        "references": noise(key_list[1], (2, ORIENT, S), (2 * S) ** -0.5, 0.03125, ((1, 4), (2, 4))),
        "noise_weight": jnp.clip(jnp.exp(math.log(3.0) - 2.3025851 * jax.random.uniform(key_list[2], (S,), jnp.float32) ** levels(key_list[2], (S,), ((0, 4),), -0.2, 0.2)), 0.3, 3.0),
        "normalizer": jnp.clip(jax.random.uniform(own_keys[3], (IMAGES,), jnp.float32, -1.0, 1.0) * levels(own_keys[3], (IMAGES,), ((0, 4),), -0.4, 0.0), -1.0, 1.0),
        "owner_order": jax.random.permutation(key_list[4], ORIENT).astype(jnp.int32),
    }


def reference(images, references, noise_weight, normalizer, owner_order):
    count = images.shape[1]
    refs = references.astype(jnp.float32)
    scaled = refs * noise_weight[None, None, :]
    weighted_refs = scaled.astype(jnp.bfloat16)
    half_power = 0.5 * lax.optimization_barrier(jnp.sum(refs * scaled, axis=(0, 2)))
    flat_images = jnp.transpose(images, (1, 0, 2)).reshape(count, 2 * S)
    flat_refs = jnp.transpose(weighted_refs, (1, 0, 2)).reshape(ORIENT, 2 * S)
    scores = jnp.dot(flat_images, flat_refs.T, preferred_element_type=jnp.float32) - half_power[None, :]
    posterior = jnp.exp(scores - normalizer[:, None]).astype(jnp.bfloat16)
    image_sums = jnp.dot(posterior.T, flat_images, preferred_element_type=jnp.float32)
    ordered = jnp.take(image_sums, owner_order.astype(jnp.int32), axis=0)
    scale_factor = 1.0 / jnp.sqrt(jnp.float32(IMAGES))
    return (ordered * scale_factor).reshape(ORIENT, 2, S).astype(jnp.bfloat16)
```

```python
import functools

import jax
import jax.numpy as jnp
from jax import lax
from jax.experimental import pallas as pl
from jax.experimental.pallas import tpu as pltpu
from jax.sharding import PartitionSpec as P

MESH = pl.DeviceIdType.MESH
F32, BF16 = jnp.float32, jnp.bfloat16


def kernel(n, nx, nc, scale, refs_hbm, images_hbm, noise, norm, order, out,
           img_v, gat, sc_send, sc_recv, post, sbuf, rbuf, own,
           img_sem, own_sem, g_send, g_recv, s_send, s_recv, p_send, p_recv, o_send, o_recv):
    ns = 2 * nx
    rows = refs_hbm.shape[1]
    orient = n * rows
    count = images_hbm.shape[1]
    ch = images_hbm.shape[2] // nc
    me = lax.axis_index("img")
    mx = lax.axis_index("samp")
    mc = lax.axis_index("sub")
    ms = mx * 2 + mc

    def cols(c):
        return pl.ds(pl.multiple_of(c * ch, ch), ch)

    def img_peer(r):
        return lax.rem(me + r, n)

    def samp_peer(r):
        t = lax.rem(ms + r, ns)
        return t, {"samp": t // 2, "sub": lax.rem(t, 2)}

    def image_copy(c, p):
        return pltpu.make_async_copy(images_hbm.at[p, :, cols(c)], img_v.at[c, p], img_sem.at[c, p])

    def own_copy(c):
        return pltpu.make_async_copy(refs_hbm.at[:, :, cols(c)], gat.at[c, me], own_sem.at[c])

    def gather_copy(c, r, slot):
        return pltpu.make_async_remote_copy(
            refs_hbm.at[:, :, cols(c)], gat.at[c, slot], g_send.at[c, r - 1], g_recv.at[c, r - 1],
            device_id={"img": img_peer(r)}, device_id_type=MESH)

    def score_copy(r):
        t, dev = samp_peer(r)
        return pltpu.make_async_remote_copy(
            sc_send.at[t], sc_recv.at[r - 1], s_send.at[r - 1], s_recv.at[r - 1],
            device_id=dev, device_id_type=MESH)

    def post_copy(r, slot):
        _, dev = samp_peer(r)
        return pltpu.make_async_remote_copy(
            post.at[slot], post.at[slot], p_send.at[r - 1], p_recv.at[r - 1],
            device_id=dev, device_id_type=MESH)

    def sum_copy(c, r):
        d = img_peer(r)
        return pltpu.make_async_remote_copy(
            sbuf.at[c, d], rbuf.at[c, r - 1], o_send.at[c, r - 1], o_recv.at[c, r - 1],
            device_id={"img": d}, device_id_type=MESH)

    barrier = pltpu.get_barrier_semaphore()
    for r in range(1, n):
        pl.semaphore_signal(barrier, inc=1, device_id={"img": img_peer(r)}, device_id_type=MESH)
    for r in range(1, ns):
        pl.semaphore_signal(barrier, inc=1, device_id=samp_peer(r)[1], device_id_type=MESH)
    for c in range(nc):
        own_copy(c).start()
        for p in range(2):
            image_copy(c, p).start()
    pl.semaphore_wait(barrier, n - 1 + ns - 1)
    for c in range(nc):
        for r in range(1, n):
            gather_copy(c, r, me).start()

    perm = (lax.broadcasted_iota(jnp.int32, (orient, orient), 1) == order[...]).astype(F32).astype(BF16)

    def score_step(c, carry):
        total, power = carry
        own_copy(c).wait()
        for p in range(2):
            image_copy(c, p).wait()
        for r in range(1, n):
            gather_copy(c, r, lax.rem(me + n - r, n)).wait_recv()
        weight = noise[:, cols(c)]
        for p in range(2):
            block = gat[c, :, p].astype(F32).reshape(orient, ch).astype(BF16)
            refs = jnp.dot(perm, block, preferred_element_type=F32)
            scaled = refs * weight
            power = power + jnp.sum(refs * scaled, axis=1, keepdims=True)
            total = total + lax.dot_general(
                scaled.astype(BF16), img_v[c, p], (((1,), (1,)), ((), ())), preferred_element_type=F32)
        return total, power

    total, power = lax.fori_loop(
        0, nc, score_step, (jnp.zeros((orient, count), F32), jnp.zeros((orient, 1), F32)))
    sc_send[...] = (total - 0.5 * power).reshape(sc_send.shape)
    for r in range(1, ns):
        score_copy(r).start()
    score = sc_send[ms]
    for r in range(1, ns):
        score_copy(r).wait_recv()
        score = score + sc_recv[r - 1]
    post[ms] = jnp.exp(score - norm[...]).astype(BF16)
    for r in range(1, ns):
        post_copy(r, ms).start()
    for r in range(1, ns):
        post_copy(r, lax.rem(ms + ns - r, ns)).wait_recv()
    weights = post[...].astype(F32).reshape(orient, count).astype(BF16)

    def sum_step(c, _):
        for p in range(2):
            sums = jnp.dot(weights, img_v[c, p], preferred_element_type=F32).reshape(n, rows, ch)
            own[c, :, p] = sums
            sbuf[c, :, p] = sums.astype(BF16)
        for r in range(1, n):
            sum_copy(c, r).start()
        return 0

    lax.fori_loop(0, nc, sum_step, 0)

    def out_step(c, _):
        value = own[c, me]
        for r in range(1, n):
            sum_copy(c, r).wait_recv()
            value = value + rbuf[c, r - 1].astype(F32)
        out[:, :, cols(c)] = (value * scale).astype(BF16)
        return 0

    lax.fori_loop(0, nc, out_step, 0)

    for r in range(1, ns):
        score_copy(r).wait_send()
        post_copy(r, ms).wait_send()

    def drain(c, _):
        for r in range(1, n):
            gather_copy(c, r, me).wait_send()
            sum_copy(c, r).wait_send()
        return 0

    lax.fori_loop(0, nc, drain, 0)


def local(images, references, noise_weight, normalizer, owner_order, *, n, nx):
    ns = 2 * nx
    _, rows, samples = references.shape
    count = images.shape[1]
    orient = n * rows
    ch = 1024
    nc = samples // ch
    scale = 1.0 / (float(count * n) ** 0.5)
    dma = pltpu.SemaphoreType.DMA
    vmem = pl.BlockSpec(memory_space=pltpu.VMEM)
    hbm = pl.BlockSpec(memory_space=pl.ANY)
    out = pl.pallas_call(
        functools.partial(kernel, n, nx, nc, scale),
        out_shape=jax.ShapeDtypeStruct((2, rows, samples), BF16),
        in_specs=[hbm, hbm, vmem, vmem, vmem],
        out_specs=vmem,
        scratch_shapes=[
            pltpu.VMEM((nc, 2, count, ch), BF16),
            pltpu.VMEM((nc, n, 2, rows, ch), BF16),
            pltpu.VMEM((ns, orient // ns, count), F32),
            pltpu.VMEM((ns - 1, orient // ns, count), F32),
            pltpu.VMEM((ns, orient // ns, count), BF16),
            pltpu.VMEM((nc, n, 2, rows, ch), BF16),
            pltpu.VMEM((nc, n - 1, 2, rows, ch), BF16),
            pltpu.VMEM((nc, n, 2, rows, ch), F32),
            dma((nc, 2)),
            dma((nc,)),
            dma((nc, n - 1)),
            dma((nc, n - 1)),
            dma((ns - 1,)),
            dma((ns - 1,)),
            dma((ns - 1,)),
            dma((ns - 1,)),
            dma((nc, n - 1)),
            dma((nc, n - 1)),
        ],
        compiler_params=pltpu.CompilerParams(
            collective_id=0, has_side_effects=True, vmem_limit_bytes=48 * 1024 * 1024),
        cost_estimate=pl.CostEstimate(
            flops=8 * orient * count * samples, bytes_accessed=4 * count * samples,
            transcendentals=orient * count),
    )(references, images, noise_weight.reshape(1, samples), normalizer.reshape(1, count),
      owner_order.reshape(orient, 1))
    return jnp.transpose(out, (1, 0, 2))


def solution(mesh):
    in_specs = (
        P(None, ("groups", "img"), ("samp", "sub")),
        P(None, "img", ("samp", "sub")),
        P(("samp", "sub")),
        P(("groups", "img")),
        P(),
    )
    out_specs = P("img", "groups", ("samp", "sub"))
    body = functools.partial(local, n=mesh.shape["img"], nx=mesh.shape["samp"])
    return jax.shard_map(body, mesh=mesh, in_specs=in_specs, out_specs=out_specs, check_vma=False)
```

```python
import functools

import jax
import jax.numpy as jnp
from jax import lax
from jax.experimental import pallas as pl
from jax.experimental.pallas import tpu as pltpu
from jax.sharding import PartitionSpec as P

MESH = pl.DeviceIdType.MESH
F32, BF16 = jnp.float32, jnp.bfloat16


def kernel(n, nx, nc, scale, refs_hbm, images_hbm, noise_hbm, norm_hbm, order_hbm, out,
           noise, norm, order, img_v, gat, sc_send, sc_recv, post, sbuf, rbuf, own,
           small_sem, img_sem, own_sem, g_send, g_recv, f_send, f_recv, s_send, s_recv, p_send, p_recv, o_send, o_recv):
    ns = 2 * nx
    rows = refs_hbm.shape[1]
    orient = n * rows
    count = images_hbm.shape[1]
    ch = images_hbm.shape[2] // nc
    me = lax.axis_index("img")
    mg = lax.axis_index("groups")
    mx = lax.axis_index("samp")
    mc = lax.axis_index("sub")
    ms = mx * 2 + mc

    def cols(c):
        return pl.ds(pl.multiple_of(c * ch, ch), ch)

    def img_peer(r):
        return lax.rem(me + r, n)

    def samp_peer(r):
        t = lax.rem(ms + r, ns)
        return t, {"samp": t // 2, "sub": lax.rem(t, 2)}

    def image_copy(c, p):
        return pltpu.make_async_copy(images_hbm.at[p, :, cols(c)], img_v.at[c, p], img_sem.at[c, p])

    def own_copy(c):
        return pltpu.make_async_copy(refs_hbm.at[:, :, cols(c)], gat.at[c, :, me], own_sem.at[c])

    def gather_copy(c, r, slot):
        return pltpu.make_async_remote_copy(
            refs_hbm.at[mg, :, cols(c)], gat.at[c, mg, slot], g_send.at[c, r - 1], g_recv.at[c, r - 1],
            device_id={"img": img_peer(r)}, device_id_type=MESH)

    def forward_copy(c, r, part):
        block = gat.at[c, part, lax.rem(me + n - r, n)]
        return pltpu.make_async_remote_copy(
            block, block, f_send.at[c, r - 1], f_recv.at[c, r - 1],
            device_id={"groups": 1 - mg}, device_id_type=MESH)

    def score_copy(r):
        t, dev = samp_peer(r)
        return pltpu.make_async_remote_copy(
            sc_send.at[t], sc_recv.at[r - 1], s_send.at[r - 1], s_recv.at[r - 1],
            device_id=dev, device_id_type=MESH)

    def post_copy(r, slot):
        _, dev = samp_peer(r)
        return pltpu.make_async_remote_copy(
            post.at[slot], post.at[slot], p_send.at[r - 1], p_recv.at[r - 1],
            device_id=dev, device_id_type=MESH)

    def sum_copy(c, r):
        d = img_peer(r)
        return pltpu.make_async_remote_copy(
            sbuf.at[c, d], rbuf.at[c, r - 1], o_send.at[c, r - 1], o_recv.at[c, r - 1],
            device_id={"img": d}, device_id_type=MESH)

    barrier = pltpu.get_barrier_semaphore()
    pl.semaphore_signal(barrier, inc=1, device_id={"groups": 1 - mg}, device_id_type=MESH)
    for r in range(1, n):
        pl.semaphore_signal(barrier, inc=1, device_id={"img": img_peer(r)}, device_id_type=MESH)
    for r in range(1, ns):
        pl.semaphore_signal(barrier, inc=1, device_id=samp_peer(r)[1], device_id_type=MESH)
    small = [pltpu.make_async_copy(a, b, small_sem.at[i]) for i, (a, b) in enumerate(
        ((order_hbm, order), (noise_hbm, noise), (norm_hbm, norm)))]
    for copy in small:
        copy.start()
    for c in range(nc):
        own_copy(c).start()
        for p in range(2):
            image_copy(c, p).start()
    pl.semaphore_wait(barrier, n + ns - 1)
    for c in range(nc):
        for r in range(1, n):
            gather_copy(c, r, me).start()

    for copy in small:
        copy.wait()
    perm = (lax.broadcasted_iota(jnp.int32, (orient, orient), 0) == order[...]).astype(F32)
    perm = perm.T.astype(BF16)

    def forward(c):
        for r in range(1, n):
            gather_copy(c, r, lax.rem(me + n - r, n)).wait_recv()
            forward_copy(c, r, mg).start()

    forward(0)

    def score_step(c, carry):
        total, power = carry

        @pl.when(c + 1 < nc)
        def _():
            forward(c + 1)

        own_copy(c).wait()
        for p in range(2):
            image_copy(c, p).wait()
        for r in range(1, n):
            forward_copy(c, r, 1 - mg).wait_recv()
        weight = noise[:, cols(c)]
        for p in range(2):
            block = gat[c, p].astype(F32).reshape(orient, ch).astype(BF16)
            refs = jnp.dot(perm, block, preferred_element_type=F32)
            scaled = refs * weight
            power = power + jnp.sum(refs * scaled, axis=1, keepdims=True)
            total = total + lax.dot_general(
                scaled.astype(BF16), img_v[c, p], (((1,), (1,)), ((), ())), preferred_element_type=F32)
        return total, power

    total, power = lax.fori_loop(
        0, nc, score_step, (jnp.zeros((orient, count), F32), jnp.zeros((orient, 1), F32)))
    sc_send[...] = (total - 0.5 * power).reshape(sc_send.shape)
    for r in range(1, ns):
        score_copy(r).start()
    score = sc_send[ms]
    for r in range(1, ns):
        score_copy(r).wait_recv()
        score = score + sc_recv[r - 1]
    post[ms] = jnp.exp(score - norm[...]).astype(BF16)
    for r in range(1, ns):
        post_copy(r, ms).start()
    for r in range(1, ns):
        post_copy(r, lax.rem(ms + ns - r, ns)).wait_recv()
    weights = post[...].astype(F32).reshape(orient, count).astype(BF16)

    def sum_step(c, _):
        for p in range(2):
            sums = jnp.dot(weights, img_v[c, p], preferred_element_type=F32).reshape(n, rows, ch)
            own[c, :, p] = sums
            sbuf[c, :, p] = sums.astype(BF16)
        for r in range(1, n):
            sum_copy(c, r).start()
        return 0

    lax.fori_loop(0, nc, sum_step, 0)

    def out_step(c, _):
        value = own[c, me]
        for r in range(1, n):
            sum_copy(c, r).wait_recv()
            value = value + rbuf[c, r - 1].astype(F32)
        out[:, :, cols(c)] = (value * scale).astype(BF16)
        return 0

    lax.fori_loop(0, nc, out_step, 0)

    for r in range(1, ns):
        score_copy(r).wait_send()
        post_copy(r, ms).wait_send()

    def drain(c, _):
        for r in range(1, n):
            gather_copy(c, r, me).wait_send()
            forward_copy(c, r, mg).wait_send()
            sum_copy(c, r).wait_send()
        return 0

    lax.fori_loop(0, nc, drain, 0)


def local(images, references, noise_weight, normalizer, owner_order, *, n, nx):
    ns = 2 * nx
    _, rows, samples = references.shape
    count = images.shape[1]
    orient = n * rows
    ch = 1024
    nc = samples // ch
    scale = 1.0 / (float(count * n) ** 0.5)
    dma = pltpu.SemaphoreType.DMA
    vmem = pl.BlockSpec(memory_space=pltpu.VMEM)
    hbm = pl.BlockSpec(memory_space=pl.ANY)
    out = pl.pallas_call(
        functools.partial(kernel, n, nx, nc, scale),
        out_shape=jax.ShapeDtypeStruct((2, rows, samples), BF16),
        in_specs=[hbm] * 5,
        out_specs=vmem,
        scratch_shapes=[
            pltpu.VMEM((1, samples), F32),
            pltpu.VMEM((1, count), F32),
            pltpu.VMEM((1, orient), jnp.int32),
            pltpu.VMEM((nc, 2, count, ch), BF16),
            pltpu.VMEM((nc, 2, n, rows, ch), BF16),
            pltpu.VMEM((ns, orient // ns, count), F32),
            pltpu.VMEM((ns - 1, orient // ns, count), F32),
            pltpu.VMEM((ns, orient // ns, count), BF16),
            pltpu.VMEM((nc, n, 2, rows, ch), BF16),
            pltpu.VMEM((nc, n - 1, 2, rows, ch), BF16),
            pltpu.VMEM((nc, n, 2, rows, ch), F32),
            dma((3,)),
            dma((nc, 2)),
            dma((nc,)),
            dma((nc, n - 1)),
            dma((nc, n - 1)),
            dma((nc, n - 1)),
            dma((nc, n - 1)),
            dma((ns - 1,)),
            dma((ns - 1,)),
            dma((ns - 1,)),
            dma((ns - 1,)),
            dma((nc, n - 1)),
            dma((nc, n - 1)),
        ],
        compiler_params=pltpu.CompilerParams(
            collective_id=0, has_side_effects=True, vmem_limit_bytes=63 * 1024 * 1024),
        cost_estimate=pl.CostEstimate(
            flops=8 * orient * count * samples, bytes_accessed=4 * count * samples,
            transcendentals=orient * count),
    )(references, images, noise_weight.reshape(1, samples), normalizer.reshape(1, count),
      owner_order.reshape(1, orient))
    return jnp.transpose(out, (1, 0, 2))


def solution(mesh):
    in_specs = (
        P(None, ("groups", "img"), ("samp", "sub")),
        P(None, "img", ("samp", "sub")),
        P(("samp", "sub")),
        P(("groups", "img")),
        P(),
    )
    out_specs = P("img", "groups", ("samp", "sub"))
    body = functools.partial(local, n=mesh.shape["img"], nx=mesh.shape["samp"])
    return jax.shard_map(body, mesh=mesh, in_specs=in_specs, out_specs=out_specs, check_vma=False)
```

```python
import functools

import jax
import jax.numpy as jnp
from jax import lax
from jax.experimental import pallas as pl
from jax.experimental.pallas import tpu as pltpu
from jax.sharding import PartitionSpec as P

MESH = pl.DeviceIdType.MESH
F32, BF16 = jnp.float32, jnp.bfloat16


def kernel(n, nx, nc, scale, refs_hbm, images_hbm, noise_hbm, norm_hbm, order_hbm, out,
           noise, norm, order, img_v, gat, sc_send, sc_recv, post, sbuf, rbuf, own,
           small_sem, img_sem, own_sem, g_send, g_recv, f_send, f_recv, s_send, s_recv, p_send, p_recv, o_send, o_recv):
    ns = 2 * nx
    rows = refs_hbm.shape[1]
    orient = n * rows
    count = images_hbm.shape[1]
    ch = images_hbm.shape[2] // nc
    me = lax.axis_index("img")
    mg = lax.axis_index("groups")
    mx = lax.axis_index("samp")
    mc = lax.axis_index("sub")
    ms = mx * 2 + mc

    def cols(c):
        return pl.ds(pl.multiple_of(c * ch, ch), ch)

    def img_peer(r):
        return lax.rem(me + r, n)

    def samp_peer(r):
        t = lax.rem(ms + r, ns)
        return t, {"samp": t // 2, "sub": lax.rem(t, 2)}

    def image_copy(c, p):
        return pltpu.make_async_copy(images_hbm.at[p, :, cols(c)], img_v.at[c, p], img_sem.at[c, p])

    def own_copy(c):
        return pltpu.make_async_copy(refs_hbm.at[:, :, cols(c)], gat.at[c, :, me], own_sem.at[c])

    def gather_copy(c, r, slot):
        return pltpu.make_async_remote_copy(
            refs_hbm.at[mg, :, cols(c)], gat.at[c, mg, slot], g_send.at[c, r - 1], g_recv.at[c, r - 1],
            device_id={"img": img_peer(r)}, device_id_type=MESH)

    def forward_copy(c, r, part):
        block = gat.at[c, part, lax.rem(me + n - r, n)]
        return pltpu.make_async_remote_copy(
            block, block, f_send.at[c, r - 1], f_recv.at[c, r - 1],
            device_id={"groups": 1 - mg}, device_id_type=MESH)

    def score_copy(r):
        t, dev = samp_peer(r)
        return pltpu.make_async_remote_copy(
            sc_send.at[t], sc_recv.at[r - 1], s_send.at[r - 1], s_recv.at[r - 1],
            device_id=dev, device_id_type=MESH)

    def post_copy(r, slot):
        _, dev = samp_peer(r)
        return pltpu.make_async_remote_copy(
            post.at[slot], post.at[slot], p_send.at[r - 1], p_recv.at[r - 1],
            device_id=dev, device_id_type=MESH)

    def sum_copy(c, r):
        d = img_peer(r)
        return pltpu.make_async_remote_copy(
            sbuf.at[c, d], rbuf.at[c, r - 1], o_send.at[c, r - 1], o_recv.at[c, r - 1],
            device_id={"img": d}, device_id_type=MESH)

    barrier = pltpu.get_barrier_semaphore()
    pl.semaphore_signal(barrier, inc=1, device_id={"groups": 1 - mg}, device_id_type=MESH)
    for r in range(1, n):
        pl.semaphore_signal(barrier, inc=1, device_id={"img": img_peer(r)}, device_id_type=MESH)
    for r in range(1, ns):
        pl.semaphore_signal(barrier, inc=1, device_id=samp_peer(r)[1], device_id_type=MESH)
    small = [pltpu.make_async_copy(a, b, small_sem.at[i]) for i, (a, b) in enumerate(
        ((order_hbm, order), (noise_hbm, noise), (norm_hbm, norm)))]
    for copy in small:
        copy.start()
    for c in range(nc):
        own_copy(c).start()
        for p in range(2):
            image_copy(c, p).start()
    pl.semaphore_wait(barrier, n + ns - 1)
    for c in range(nc):
        for r in range(1, n):
            gather_copy(c, r, me).start()

    for copy in small:
        copy.wait()
    perm = (lax.broadcasted_iota(jnp.int32, (orient, orient), 0) == order[...]).astype(F32)
    perm = perm.T.astype(BF16)

    def forward(c):
        for r in range(1, n):
            gather_copy(c, r, lax.rem(me + n - r, n)).wait_recv()
            forward_copy(c, r, mg).start()

    forward(0)

    def score_step(c, carry):
        total, power = carry

        @pl.when(c + 1 < nc)
        def _():
            forward(c + 1)

        own_copy(c).wait()
        for p in range(2):
            image_copy(c, p).wait()
        for r in range(1, n):
            forward_copy(c, r, 1 - mg).wait_recv()
        weight = noise[:, cols(c)]
        for p in range(2):
            block = gat[c, p].astype(F32).reshape(orient, ch).astype(BF16)
            refs = jnp.dot(perm, block, preferred_element_type=F32)
            scaled = refs * weight
            power = power + jnp.sum(refs * scaled, axis=1, keepdims=True)
            total = total + lax.dot_general(
                scaled.astype(BF16), img_v[c, p], (((1,), (1,)), ((), ())), preferred_element_type=F32)
        return total, power

    total, power = lax.fori_loop(
        0, nc, score_step, (jnp.zeros((orient, count), F32), jnp.zeros((orient, 1), F32)))
    sc_send[...] = (total - 0.5 * power).reshape(sc_send.shape)
    for r in range(1, ns):
        score_copy(r).start()
    score = sc_send[ms]
    for r in range(1, ns):
        score_copy(r).wait_recv()
        score = score + sc_recv[r - 1]
    post[ms] = jnp.exp(score - norm[...]).astype(BF16)
    for r in range(1, ns):
        post_copy(r, ms).start()
    for r in range(1, ns):
        post_copy(r, lax.rem(ms + ns - r, ns)).wait_recv()
    weights = post[...].astype(F32).reshape(orient, count).astype(BF16)

    def local_sums(c):
        for p in range(2):
            own[c, :, p] = jnp.dot(
                weights, img_v[c, p], preferred_element_type=F32).reshape(n, rows, ch)

    def emit(c, value):
        out[:, :, cols(c)] = (value * scale).astype(BF16)

    if n == 4:
        end = jnp.logical_or(me == 0, me == 3)
        low = me < 2
        other = 3 - me
        near = lax.select(end, lax.select(low, 1, 2), lax.select(low, 0, 3))
        far = 3 - near

        def hop(c, block, slot, to):
            return pltpu.make_async_remote_copy(
                sbuf.at[c, block], rbuf.at[c, slot], o_send.at[c, slot], o_recv.at[c, slot],
                device_id={"img": to}, device_id_type=MESH)

        @pl.when(end)
        def _():
            def first(c, _):
                local_sums(c)
                sbuf[c] = own[c].astype(BF16)
                hop(c, other, 0, near).start()
                return 0

            def second(c, _):
                hop(c, far, 1, near).start()
                return 0

            def third(c, _):
                hop(c, near, 2, near).start()
                return 0

            def last(c, _):
                hop(c, other, 0, near).wait_recv()
                emit(c, own[c, me] + rbuf[c, 0].astype(F32))
                return 0

            def drained(c, _):
                hop(c, other, 0, near).wait_send()
                hop(c, far, 1, near).wait_send()
                hop(c, near, 2, near).wait_send()
                return 0

            for step in (first, second, third, last, drained):
                lax.fori_loop(0, nc, step, 0)

        @pl.when(jnp.logical_not(end))
        def _():
            def add(c, block, slot):
                hop(c, block, slot, other).wait_recv()
                sbuf[c, block] = (own[c, block] + rbuf[c, slot].astype(F32)).astype(BF16)

            def first(c, _):
                local_sums(c)
                add(c, far, 0)
                hop(c, far, 3, other).start()
                return 0

            def second(c, _):
                add(c, near, 3)
                hop(c, near, 0, near).start()
                return 0

            def third(c, _):
                add(c, other, 1)
                hop(c, other, 4, other).start()
                return 0

            def last(c, _):
                hop(c, other, 2, other).wait_recv()
                hop(c, other, 4, other).wait_recv()
                emit(c, own[c, me] + rbuf[c, 2].astype(F32) + rbuf[c, 4].astype(F32))
                return 0

            def drained(c, _):
                hop(c, far, 3, other).wait_send()
                hop(c, near, 0, near).wait_send()
                hop(c, other, 4, other).wait_send()
                return 0

            for step in (first, second, third, last, drained):
                lax.fori_loop(0, nc, step, 0)
    else:
        def sum_step(c, _):
            local_sums(c)
            sbuf[c] = own[c].astype(BF16)
            for r in range(1, n):
                sum_copy(c, r).start()
            return 0

        def out_step(c, _):
            value = own[c, me]
            for r in range(1, n):
                sum_copy(c, r).wait_recv()
                value = value + rbuf[c, r - 1].astype(F32)
            emit(c, value)
            for r in range(1, n):
                sum_copy(c, r).wait_send()
            return 0

        lax.fori_loop(0, nc, sum_step, 0)
        lax.fori_loop(0, nc, out_step, 0)

    for r in range(1, ns):
        score_copy(r).wait_send()
        post_copy(r, ms).wait_send()

    def drain(c, _):
        for r in range(1, n):
            gather_copy(c, r, me).wait_send()
            forward_copy(c, r, mg).wait_send()
        return 0

    lax.fori_loop(0, nc, drain, 0)


def local(images, references, noise_weight, normalizer, owner_order, *, n, nx):
    ns = 2 * nx
    _, rows, samples = references.shape
    count = images.shape[1]
    orient = n * rows
    ch = 1024
    nc = samples // ch
    slots = 5 if n == 4 else n - 1
    scale = 1.0 / (float(count * n) ** 0.5)
    dma = pltpu.SemaphoreType.DMA
    vmem = pl.BlockSpec(memory_space=pltpu.VMEM)
    hbm = pl.BlockSpec(memory_space=pl.ANY)
    out = pl.pallas_call(
        functools.partial(kernel, n, nx, nc, scale),
        out_shape=jax.ShapeDtypeStruct((2, rows, samples), BF16),
        in_specs=[hbm] * 5,
        out_specs=vmem,
        scratch_shapes=[
            pltpu.VMEM((1, samples), F32),
            pltpu.VMEM((1, count), F32),
            pltpu.VMEM((1, orient), jnp.int32),
            pltpu.VMEM((nc, 2, count, ch), BF16),
            pltpu.VMEM((nc, 2, n, rows, ch), BF16),
            pltpu.VMEM((ns, orient // ns, count), F32),
            pltpu.VMEM((ns - 1, orient // ns, count), F32),
            pltpu.VMEM((ns, orient // ns, count), BF16),
            pltpu.VMEM((nc, n, 2, rows, ch), BF16),
            pltpu.VMEM((nc, slots, 2, rows, ch), BF16),
            pltpu.VMEM((nc, n, 2, rows, ch), F32),
            dma((3,)),
            dma((nc, 2)),
            dma((nc,)),
            dma((nc, n - 1)),
            dma((nc, n - 1)),
            dma((nc, n - 1)),
            dma((nc, n - 1)),
            dma((ns - 1,)),
            dma((ns - 1,)),
            dma((ns - 1,)),
            dma((ns - 1,)),
            dma((nc, slots)),
            dma((nc, slots)),
        ],
        compiler_params=pltpu.CompilerParams(
            collective_id=0, has_side_effects=True, vmem_limit_bytes=63 * 1024 * 1024),
        cost_estimate=pl.CostEstimate(
            flops=8 * orient * count * samples, bytes_accessed=4 * count * samples,
            transcendentals=orient * count),
    )(references, images, noise_weight.reshape(1, samples), normalizer.reshape(1, count),
      owner_order.reshape(1, orient))
    return jnp.transpose(out, (1, 0, 2))


def solution(mesh):
    in_specs = (
        P(None, ("groups", "img"), ("samp", "sub")),
        P(None, "img", ("samp", "sub")),
        P(("samp", "sub")),
        P(("groups", "img")),
        P(),
    )
    out_specs = P("img", "groups", ("samp", "sub"))
    body = functools.partial(local, n=mesh.shape["img"], nx=mesh.shape["samp"])
    return jax.shard_map(body, mesh=mesh, in_specs=in_specs, out_specs=out_specs, check_vma=False)
```

```python
import functools

import jax
import jax.numpy as jnp
from jax import lax
from jax.experimental import pallas as pl
from jax.experimental.pallas import tpu as pltpu
from jax.sharding import PartitionSpec as P

MESH = pl.DeviceIdType.MESH
F32, BF16 = jnp.float32, jnp.bfloat16


def kernel(n, nx, nc, scale, refs_hbm, images_hbm, noise_hbm, norm_hbm, order_hbm, out,
           noise, norm, order, img_v, gat, sc_send, sc_recv, post, sbuf, rbuf, own,
           small_sem, img_sem, own_sem, g_send, g_recv, f_send, f_recv, s_send, s_recv, p_send, p_recv, o_send, o_recv):
    ns = 2 * nx
    rows = refs_hbm.shape[1]
    orient = n * rows
    count = images_hbm.shape[1]
    ch = images_hbm.shape[2] // nc
    me = lax.axis_index("img")
    mg = lax.axis_index("groups")
    mx = lax.axis_index("samp")
    mc = lax.axis_index("sub")
    ms = mx * 2 + mc

    def cols(c):
        return pl.ds(pl.multiple_of(c * ch, ch), ch)

    def img_peer(r):
        return lax.rem(me + r, n)

    def samp_peer(r):
        t = lax.rem(ms + r, ns)
        return t, {"samp": t // 2, "sub": lax.rem(t, 2)}

    def image_copy(c, p):
        return pltpu.make_async_copy(images_hbm.at[p, :, cols(c)], img_v.at[c, p], img_sem.at[c, p])

    def own_copy(c):
        return pltpu.make_async_copy(refs_hbm.at[mg, :, cols(c)], gat.at[c, mg, me], own_sem.at[c])

    def gather_copy(c, r, slot):
        return pltpu.make_async_remote_copy(
            refs_hbm.at[mg, :, cols(c)], gat.at[c, mg, slot], g_send.at[c, r - 1], g_recv.at[c, r - 1],
            device_id={"img": img_peer(r)}, device_id_type=MESH)

    def forward_copy(c, part):
        block = gat.at[c, part]
        return pltpu.make_async_remote_copy(
            block, block, f_send.at[c], f_recv.at[c],
            device_id={"groups": 1 - mg}, device_id_type=MESH)

    def score_copy(r):
        t, dev = samp_peer(r)
        return pltpu.make_async_remote_copy(
            sc_send.at[t], sc_recv.at[r - 1], s_send.at[r - 1], s_recv.at[r - 1],
            device_id=dev, device_id_type=MESH)

    def post_copy(r, slot):
        _, dev = samp_peer(r)
        return pltpu.make_async_remote_copy(
            post.at[slot], post.at[slot], p_send.at[r - 1], p_recv.at[r - 1],
            device_id=dev, device_id_type=MESH)

    def sum_copy(c, r):
        d = img_peer(r)
        return pltpu.make_async_remote_copy(
            sbuf.at[c, d], rbuf.at[c, r - 1], o_send.at[c, r - 1], o_recv.at[c, r - 1],
            device_id={"img": d}, device_id_type=MESH)

    barrier = pltpu.get_barrier_semaphore()
    pl.semaphore_signal(barrier, inc=1, device_id={"groups": 1 - mg}, device_id_type=MESH)
    for r in range(1, n):
        pl.semaphore_signal(barrier, inc=1, device_id={"img": img_peer(r)}, device_id_type=MESH)
    for r in range(1, ns):
        pl.semaphore_signal(barrier, inc=1, device_id=samp_peer(r)[1], device_id_type=MESH)
    small = [pltpu.make_async_copy(a, b, small_sem.at[i]) for i, (a, b) in enumerate(
        ((order_hbm, order), (noise_hbm, noise), (norm_hbm, norm)))]
    for copy in small:
        copy.start()
    for c in range(nc):
        own_copy(c).start()
        for p in range(2):
            image_copy(c, p).start()
    pl.semaphore_wait(barrier, n + ns - 1)
    for c in range(nc):
        for r in range(1, n):
            gather_copy(c, r, me).start()

    for copy in small:
        copy.wait()
    perm = (lax.broadcasted_iota(jnp.int32, (orient, orient), 0) == order[...]).astype(F32)
    perm = perm.T.astype(BF16)

    def score(c, p, carry):
        total, power = carry
        image_copy(c, p).wait()
        block = gat[c, p].astype(F32).reshape(orient, ch).astype(BF16)
        refs = jnp.dot(perm, block, preferred_element_type=F32)
        scaled = refs * noise[:, cols(c)]
        power = power + jnp.sum(refs * scaled, axis=1, keepdims=True)
        total = total + lax.dot_general(
            scaled.astype(BF16), img_v[c, p], (((1,), (1,)), ((), ())), preferred_element_type=F32)
        return total, power

    def gathered(c, carry):
        own_copy(c).wait()
        for r in range(1, n):
            gather_copy(c, r, lax.rem(me + n - r, n)).wait_recv()
        forward_copy(c, mg).start()
        return score(c, mg, carry)

    def forwarded(c, carry):
        forward_copy(c, 1 - mg).wait_recv()
        return score(c, 1 - mg, carry)

    carry = (jnp.zeros((orient, count), F32), jnp.zeros((orient, 1), F32))
    carry = lax.fori_loop(0, nc, gathered, carry)
    total, power = lax.fori_loop(0, nc, forwarded, carry)
    sc_send[...] = (total - 0.5 * power).reshape(sc_send.shape)
    for r in range(1, ns):
        score_copy(r).start()
    row = sc_send[ms]
    for r in range(1, ns):
        score_copy(r).wait_recv()
        row = row + sc_recv[r - 1]
    post[ms] = jnp.exp(row - norm[...]).astype(BF16)
    for r in range(1, ns):
        post_copy(r, ms).start()
    for r in range(1, ns):
        post_copy(r, lax.rem(ms + ns - r, ns)).wait_recv()
    weights = post[...].astype(F32).reshape(orient, count).astype(BF16)

    def local_sums(c):
        for p in range(2):
            own[c, :, p] = jnp.dot(
                weights, img_v[c, p], preferred_element_type=F32).reshape(n, rows, ch)

    def emit(c, value):
        out[:, :, cols(c)] = (value * scale).astype(BF16)

    if n == 4:
        end = jnp.logical_or(me == 0, me == 3)
        low = me < 2
        other = 3 - me
        near = lax.select(end, lax.select(low, 1, 2), lax.select(low, 0, 3))
        far = 3 - near

        def hop(c, block, slot, to):
            return pltpu.make_async_remote_copy(
                sbuf.at[c, block], rbuf.at[c, slot], o_send.at[c, slot], o_recv.at[c, slot],
                device_id={"img": to}, device_id_type=MESH)

        @pl.when(end)
        def _():
            def first(c, _):
                local_sums(c)
                sbuf[c] = own[c].astype(BF16)
                hop(c, other, 0, near).start()
                return 0

            def second(c, _):
                hop(c, far, 1, near).start()
                return 0

            def third(c, _):
                hop(c, near, 2, near).start()
                return 0

            def last(c, _):
                hop(c, other, 0, near).wait_recv()
                emit(c, own[c, me] + rbuf[c, 0].astype(F32))
                return 0

            def drained(c, _):
                hop(c, other, 0, near).wait_send()
                hop(c, far, 1, near).wait_send()
                hop(c, near, 2, near).wait_send()
                return 0

            for step in (first, second, third, last, drained):
                lax.fori_loop(0, nc, step, 0)

        @pl.when(jnp.logical_not(end))
        def _():
            def add(c, block, slot):
                hop(c, block, slot, other).wait_recv()
                sbuf[c, block] = (own[c, block] + rbuf[c, slot].astype(F32)).astype(BF16)

            def first(c, _):
                local_sums(c)
                add(c, far, 0)
                hop(c, far, 3, other).start()
                return 0

            def second(c, _):
                add(c, near, 3)
                hop(c, near, 0, near).start()
                return 0

            def third(c, _):
                add(c, other, 1)
                hop(c, other, 4, other).start()
                return 0

            def last(c, _):
                hop(c, other, 2, other).wait_recv()
                hop(c, other, 4, other).wait_recv()
                emit(c, own[c, me] + rbuf[c, 2].astype(F32) + rbuf[c, 4].astype(F32))
                return 0

            def drained(c, _):
                hop(c, far, 3, other).wait_send()
                hop(c, near, 0, near).wait_send()
                hop(c, other, 4, other).wait_send()
                return 0

            for step in (first, second, third, last, drained):
                lax.fori_loop(0, nc, step, 0)
    else:
        def sum_step(c, _):
            local_sums(c)
            sbuf[c] = own[c].astype(BF16)
            for r in range(1, n):
                sum_copy(c, r).start()
            return 0

        def out_step(c, _):
            value = own[c, me]
            for r in range(1, n):
                sum_copy(c, r).wait_recv()
                value = value + rbuf[c, r - 1].astype(F32)
            emit(c, value)
            for r in range(1, n):
                sum_copy(c, r).wait_send()
            return 0

        lax.fori_loop(0, nc, sum_step, 0)
        lax.fori_loop(0, nc, out_step, 0)

    for r in range(1, ns):
        score_copy(r).wait_send()
        post_copy(r, ms).wait_send()

    def drain(c, _):
        for r in range(1, n):
            gather_copy(c, r, me).wait_send()
        forward_copy(c, mg).wait_send()
        return 0

    lax.fori_loop(0, nc, drain, 0)


def local(images, references, noise_weight, normalizer, owner_order, *, n, nx):
    ns = 2 * nx
    _, rows, samples = references.shape
    count = images.shape[1]
    orient = n * rows
    ch = min(1024, samples)
    nc = samples // ch
    slots = 5 if n == 4 else n - 1
    scale = 1.0 / (float(count * n) ** 0.5)
    dma = pltpu.SemaphoreType.DMA
    vmem = pl.BlockSpec(memory_space=pltpu.VMEM)
    hbm = pl.BlockSpec(memory_space=pl.ANY)
    out = pl.pallas_call(
        functools.partial(kernel, n, nx, nc, scale),
        out_shape=jax.ShapeDtypeStruct((2, rows, samples), BF16),
        in_specs=[hbm] * 5,
        out_specs=vmem,
        scratch_shapes=[
            pltpu.VMEM((1, samples), F32),
            pltpu.VMEM((1, count), F32),
            pltpu.VMEM((1, orient), jnp.int32),
            pltpu.VMEM((nc, 2, count, ch), BF16),
            pltpu.VMEM((nc, 2, n, rows, ch), BF16),
            pltpu.VMEM((ns, orient // ns, count), F32),
            pltpu.VMEM((ns - 1, orient // ns, count), F32),
            pltpu.VMEM((ns, orient // ns, count), BF16),
            pltpu.VMEM((nc, n, 2, rows, ch), BF16),
            pltpu.VMEM((nc, slots, 2, rows, ch), BF16),
            pltpu.VMEM((nc, n, 2, rows, ch), F32),
            dma((3,)),
            dma((nc, 2)),
            dma((nc,)),
            dma((nc, n - 1)),
            dma((nc, n - 1)),
            dma((nc,)),
            dma((nc,)),
            dma((ns - 1,)),
            dma((ns - 1,)),
            dma((ns - 1,)),
            dma((ns - 1,)),
            dma((nc, slots)),
            dma((nc, slots)),
        ],
        compiler_params=pltpu.CompilerParams(
            collective_id=0, has_side_effects=True, vmem_limit_bytes=63 * 1024 * 1024),
        cost_estimate=pl.CostEstimate(
            flops=8 * orient * count * samples, bytes_accessed=4 * count * samples,
            transcendentals=orient * count),
    )(references, images, noise_weight.reshape(1, samples), normalizer.reshape(1, count),
      owner_order.reshape(1, orient))
    return jnp.transpose(out, (1, 0, 2))


def solution(mesh):
    in_specs = (
        P(None, ("groups", "img"), ("samp", "sub")),
        P(None, "img", ("samp", "sub")),
        P(("samp", "sub")),
        P(("groups", "img")),
        P(),
    )
    out_specs = P("img", "groups", ("samp", "sub"))
    body = functools.partial(local, n=mesh.shape["img"], nx=mesh.shape["samp"])
    return jax.shard_map(body, mesh=mesh, in_specs=in_specs, out_specs=out_specs, check_vma=False)
```

```python
import functools

import jax
import jax.numpy as jnp
from jax import lax
from jax.experimental import pallas as pl
from jax.experimental.pallas import tpu as pltpu
from jax.sharding import PartitionSpec as P

MESH = pl.DeviceIdType.MESH
F32, BF16 = jnp.float32, jnp.bfloat16


def kernel(n, nx, nc, scale, refs_hbm, images_hbm, noise_hbm, norm_hbm, order_hbm, out,
           noise, norm, order, img_v, gat, parts, sbuf, rbuf, own,
           small_sem, img_sem, own_sem, g_send, g_recv, f_send, f_recv, s_send, s_recv, o_send, o_recv):
    ns = 2 * nx
    rows = refs_hbm.shape[1]
    orient = n * rows
    count = images_hbm.shape[1]
    ch = images_hbm.shape[2] // nc
    me = lax.axis_index("img")
    mg = lax.axis_index("groups")
    mx = lax.axis_index("samp")
    mc = lax.axis_index("sub")
    ms = mx * 2 + mc

    def cols(c):
        return pl.ds(pl.multiple_of(c * ch, ch), ch)

    def img_peer(r):
        return lax.rem(me + r, n)

    def samp_peer(r):
        t = lax.rem(ms + r, ns)
        return {"samp": t // 2, "sub": lax.rem(t, 2)}

    def image_copy(c, p):
        return pltpu.make_async_copy(images_hbm.at[p, :, cols(c)], img_v.at[c, p], img_sem.at[c, p])

    def own_copy(c):
        return pltpu.make_async_copy(refs_hbm.at[mg, :, cols(c)], gat.at[c, mg, me], own_sem.at[c])

    def gather_copy(c, r, slot):
        return pltpu.make_async_remote_copy(
            refs_hbm.at[mg, :, cols(c)], gat.at[c, mg, slot], g_send.at[c, r - 1], g_recv.at[c, r - 1],
            device_id={"img": img_peer(r)}, device_id_type=MESH)

    def forward_copy(c, part):
        block = gat.at[c, part]
        return pltpu.make_async_remote_copy(
            block, block, f_send.at[c], f_recv.at[c],
            device_id={"groups": 1 - mg}, device_id_type=MESH)

    def score_copy(r, slot):
        return pltpu.make_async_remote_copy(
            parts.at[slot], parts.at[slot], s_send.at[r - 1], s_recv.at[r - 1],
            device_id=samp_peer(r), device_id_type=MESH)

    def sum_copy(c, r):
        d = img_peer(r)
        return pltpu.make_async_remote_copy(
            sbuf.at[c, d], rbuf.at[c, r - 1], o_send.at[c, r - 1], o_recv.at[c, r - 1],
            device_id={"img": d}, device_id_type=MESH)

    barrier = pltpu.get_barrier_semaphore()
    pl.semaphore_signal(barrier, inc=1, device_id={"groups": 1 - mg}, device_id_type=MESH)
    for r in range(1, n):
        pl.semaphore_signal(barrier, inc=1, device_id={"img": img_peer(r)}, device_id_type=MESH)
    for r in range(1, ns):
        pl.semaphore_signal(barrier, inc=1, device_id=samp_peer(r), device_id_type=MESH)
    small = [pltpu.make_async_copy(a, b, small_sem.at[i]) for i, (a, b) in enumerate(
        ((order_hbm, order), (noise_hbm, noise), (norm_hbm, norm)))]
    for copy in small:
        copy.start()
    for c in range(nc):
        own_copy(c).start()
        for p in range(2):
            image_copy(c, p).start()
    pl.semaphore_wait(barrier, n + ns - 1)
    for c in range(nc):
        for r in range(1, n):
            gather_copy(c, r, me).start()

    for copy in small:
        copy.wait()
    perm = (lax.broadcasted_iota(jnp.int32, (orient, orient), 0) == order[...]).astype(F32)
    perm = perm.T.astype(BF16)

    def score(c, p, carry):
        total, power = carry
        image_copy(c, p).wait()
        block = gat[c, p].astype(F32).reshape(orient, ch).astype(BF16)
        refs = jnp.dot(perm, block, preferred_element_type=F32)
        scaled = refs * noise[:, cols(c)]
        power = power + jnp.sum(refs * scaled, axis=1, keepdims=True)
        total = total + lax.dot_general(
            scaled.astype(BF16), img_v[c, p], (((1,), (1,)), ((), ())), preferred_element_type=F32)
        return total, power

    def gathered(c, carry):
        own_copy(c).wait()
        for r in range(1, n):
            gather_copy(c, r, lax.rem(me + n - r, n)).wait_recv()
        forward_copy(c, mg).start()
        return score(c, mg, carry)

    def forwarded(c, carry):
        forward_copy(c, 1 - mg).wait_recv()
        return score(c, 1 - mg, carry)

    carry = (jnp.zeros((orient, count), F32), jnp.zeros((orient, 1), F32))
    carry = lax.fori_loop(0, nc, gathered, carry)
    total, power = lax.fori_loop(0, nc, forwarded, carry)
    parts[ms] = total - 0.5 * power
    for r in range(1, ns):
        score_copy(r, ms).start()
    for r in range(1, ns):
        score_copy(r, lax.rem(ms + ns - r, ns)).wait_recv()
    scores = parts[0]
    for i in range(1, ns):
        scores = scores + parts[i]
    weights = jnp.exp(scores - norm[...]).astype(BF16)

    def local_sums(c):
        for p in range(2):
            own[c, :, p] = jnp.dot(
                weights, img_v[c, p], preferred_element_type=F32).reshape(n, rows, ch)

    def emit(c, value):
        out[:, :, cols(c)] = (value * scale).astype(BF16)

    if n == 4:
        end = jnp.logical_or(me == 0, me == 3)
        low = me < 2
        other = 3 - me
        near = lax.select(end, lax.select(low, 1, 2), lax.select(low, 0, 3))
        far = 3 - near

        def hop(c, block, slot, to):
            return pltpu.make_async_remote_copy(
                sbuf.at[c, block], rbuf.at[c, slot], o_send.at[c, slot], o_recv.at[c, slot],
                device_id={"img": to}, device_id_type=MESH)

        @pl.when(end)
        def _():
            def first(c, _):
                local_sums(c)
                sbuf[c] = own[c].astype(BF16)
                hop(c, other, 0, near).start()
                return 0

            def second(c, _):
                hop(c, far, 1, near).start()
                return 0

            def third(c, _):
                hop(c, near, 2, near).start()
                return 0

            def last(c, _):
                hop(c, other, 0, near).wait_recv()
                emit(c, own[c, me] + rbuf[c, 0].astype(F32))
                return 0

            def drained(c, _):
                hop(c, other, 0, near).wait_send()
                hop(c, far, 1, near).wait_send()
                hop(c, near, 2, near).wait_send()
                return 0

            for step in (first, second, third, last, drained):
                lax.fori_loop(0, nc, step, 0)

        @pl.when(jnp.logical_not(end))
        def _():
            def add(c, block, slot):
                hop(c, block, slot, other).wait_recv()
                sbuf[c, block] = (own[c, block] + rbuf[c, slot].astype(F32)).astype(BF16)

            def first(c, _):
                local_sums(c)
                add(c, far, 0)
                hop(c, far, 3, other).start()
                return 0

            def second(c, _):
                add(c, near, 3)
                hop(c, near, 0, near).start()
                return 0

            def third(c, _):
                add(c, other, 1)
                hop(c, other, 4, other).start()
                return 0

            def last(c, _):
                hop(c, other, 2, other).wait_recv()
                hop(c, other, 4, other).wait_recv()
                emit(c, own[c, me] + rbuf[c, 2].astype(F32) + rbuf[c, 4].astype(F32))
                return 0

            def drained(c, _):
                hop(c, far, 3, other).wait_send()
                hop(c, near, 0, near).wait_send()
                hop(c, other, 4, other).wait_send()
                return 0

            for step in (first, second, third, last, drained):
                lax.fori_loop(0, nc, step, 0)
    else:
        def sum_step(c, _):
            local_sums(c)
            sbuf[c] = own[c].astype(BF16)
            for r in range(1, n):
                sum_copy(c, r).start()
            return 0

        def out_step(c, _):
            value = own[c, me]
            for r in range(1, n):
                sum_copy(c, r).wait_recv()
                value = value + rbuf[c, r - 1].astype(F32)
            emit(c, value)
            for r in range(1, n):
                sum_copy(c, r).wait_send()
            return 0

        lax.fori_loop(0, nc, sum_step, 0)
        lax.fori_loop(0, nc, out_step, 0)

    for r in range(1, ns):
        score_copy(r, ms).wait_send()

    def drain(c, _):
        for r in range(1, n):
            gather_copy(c, r, me).wait_send()
        forward_copy(c, mg).wait_send()
        return 0

    lax.fori_loop(0, nc, drain, 0)


def local(images, references, noise_weight, normalizer, owner_order, *, n, nx):
    ns = 2 * nx
    _, rows, samples = references.shape
    count = images.shape[1]
    orient = n * rows
    ch = min(1024, samples)
    nc = samples // ch
    slots = 5 if n == 4 else n - 1
    scale = 1.0 / (float(count * n) ** 0.5)
    dma = pltpu.SemaphoreType.DMA
    vmem = pl.BlockSpec(memory_space=pltpu.VMEM)
    hbm = pl.BlockSpec(memory_space=pl.ANY)
    out = pl.pallas_call(
        functools.partial(kernel, n, nx, nc, scale),
        out_shape=jax.ShapeDtypeStruct((2, rows, samples), BF16),
        in_specs=[hbm] * 5,
        out_specs=vmem,
        scratch_shapes=[
            pltpu.VMEM((1, samples), F32),
            pltpu.VMEM((1, count), F32),
            pltpu.VMEM((1, orient), jnp.int32),
            pltpu.VMEM((nc, 2, count, ch), BF16),
            pltpu.VMEM((nc, 2, n, rows, ch), BF16),
            pltpu.VMEM((ns, orient, count), F32),
            pltpu.VMEM((nc, n, 2, rows, ch), BF16),
            pltpu.VMEM((nc, slots, 2, rows, ch), BF16),
            pltpu.VMEM((nc, n, 2, rows, ch), F32),
            dma((3,)),
            dma((nc, 2)),
            dma((nc,)),
            dma((nc, n - 1)),
            dma((nc, n - 1)),
            dma((nc,)),
            dma((nc,)),
            dma((ns - 1,)),
            dma((ns - 1,)),
            dma((nc, slots)),
            dma((nc, slots)),
        ],
        compiler_params=pltpu.CompilerParams(
            collective_id=0, has_side_effects=True, vmem_limit_bytes=63 * 1024 * 1024),
        cost_estimate=pl.CostEstimate(
            flops=8 * orient * count * samples, bytes_accessed=4 * count * samples,
            transcendentals=orient * count),
    )(references, images, noise_weight.reshape(1, samples), normalizer.reshape(1, count),
      owner_order.reshape(1, orient))
    return jnp.transpose(out, (1, 0, 2))


def solution(mesh):
    in_specs = (
        P(None, ("groups", "img"), ("samp", "sub")),
        P(None, "img", ("samp", "sub")),
        P(("samp", "sub")),
        P(("groups", "img")),
        P(),
    )
    out_specs = P("img", "groups", ("samp", "sub"))
    body = functools.partial(local, n=mesh.shape["img"], nx=mesh.shape["samp"])
    return jax.shard_map(body, mesh=mesh, in_specs=in_specs, out_specs=out_specs, check_vma=False)
```
